32 devices in a mesh: branch: 2 (over core), seq: 16 (over z, y, x).
Axes of the slice: x: 2, y: 2, z: 4, core: 2. Of those that a mesh axis runs over, the one named last changes fastest.
Arguments:
- hidden: bfloat16 [2, 12288, 1024], P('branch', 'seq')
- noisy_mel_state: float32 [100, 12288], P(None, 'seq'), may hold values from -6 to 6
- modulation: float32 [5, 1024], replicated, may hold values from -3 to 3
- feedforward_in_weight: bfloat16 [1024, 2048], replicated, may hold values from -0.1875 to 0.1875
- feedforward_in_bias: float32 [2048], replicated, may hold values from -1.75 to 1.75
- feedforward_out_weight: bfloat16 [2048, 1024], replicated, may hold values from -0.125 to 0.125
- feedforward_out_bias: float32 [1024], replicated, may hold values from -1.75 to 1.75
- mel_velocity_weight: bfloat16 [1024, 100], replicated, may hold values from -0.1875 to 0.1875
- mel_velocity_bias: float32 [100], replicated, may hold values from -3 to 3
- input_conv_weight: bfloat16 [700, 512], replicated, may hold values from -0.21875 to 0.21875
- input_conv_bias: float32 [512], replicated, may hold values from -1.75 to 1.75
- transposed_conv_weight: bfloat16 [4096, 512], replicated, may hold values from -0.1875 to 0.1875
- transposed_conv_bias: float32 [256], replicated, may hold values from -1.75 to 1.75
- snake_freq_first: float32 [256], replicated, may hold values from 0.5 to 3
- dilated_conv_weight: bfloat16 [768, 256], replicated, may hold values from -0.21875 to 0.21875
- dilated_conv_bias: float32 [256], replicated, may hold values from -1.75 to 1.75
- snake_freq_second: float32 [256], replicated, may hold values from 0.5 to 3
- second_conv_weight: bfloat16 [768, 256], replicated, may hold values from -0.21875 to 0.21875
- second_conv_bias: float32 [256], replicated, may hold values from -1.75 to 1.75
- frame_holder: int32 [12288], P('seq'), may hold values from 0 to 31, as said below
- frame_position: int32 [12288], P('seq'), may hold values from 0 to 767, as said below
- holder_utterance_length: int32 [32], replicated, may hold values from 1 to 768, as said below
Outputs:
- wave: bfloat16 [32, 256, 6144], P(('branch', 'seq'))
The draws below stay inside these ranges and needn't reach their ends.
Inputs may be any that keep to these rules, and one draw needn't show every extreme that they name: `frame_holder`: the frames form 32 utterances, each a run of consecutive frames; all frames of an utterance name one owner, and each owner is named by exactly one utterance. `frame_position`: A frame's position in its utterance, 0 at the utterance's first frame. `holder_utterance_length`: the number of frames that name the owner; every utterance has at least one frame.
All inputs are finite; a program needn't handle non-finite values.
Results may differ from the reference program's by a relative error of at most 0.015.
Values may be sent and summed in bfloat16 or wider, within the bound.
A program may use at most 128 MiB of HBM per device.

```python
import math
import jax
import jax.numpy as jnp
from jax import lax

D = 1024
FF = 2048
BINS = 100
CH0 = 512
UPSAMPLED_CHANS = 256
UP = 8
KT = 16
KPRE = 7
DILATION_RATE = 3
NFE = 16
F_DEV = 768
FRAMES = 12288
OWNERS = 32
MOST = 768
N_SEQ = 16


def utterance_layout(key):
    base_key = jax.random.fold_in(key, 11)
    pick_key, order_key, mix_key = jax.random.split(base_key, 3)
    longest = jax.random.randint(pick_key, (), 0, OWNERS)
    spare_frames = FRAMES - MOST
    even_share = spare_frames // (OWNERS - 1)
    leftover = spare_frames % (OWNERS - 1)
    indices = jnp.arange(OWNERS)
    others_rank = indices - (indices > longest).astype(jnp.int32)
    lengths = jnp.where(indices == longest, MOST, even_share + (others_rank < leftover).astype(jnp.int32))
    for mix_step in range(8):
        pair_key, amount_key = jax.random.split(jax.random.fold_in(mix_key, mix_step))
        shuffled = jax.random.permutation(pair_key, OWNERS)
        first_of = shuffled[0::2]
        second_of = shuffled[1::2]
        blocked = (first_of == longest) | (second_of == longest)
        pair_sum = lengths[first_of] + lengths[second_of]
        low_bound = jnp.maximum(1, pair_sum - MOST)
        high_bound = jnp.minimum(MOST, pair_sum - 1)
        new_first = jax.random.randint(amount_key, first_of.shape, low_bound, high_bound + 1)
        new_first = jnp.where(blocked, lengths[first_of], new_first)
        lengths = lengths.at[first_of].set(new_first).at[second_of].set(pair_sum - new_first)
    starts = jnp.cumsum(lengths) - lengths
    assign = jax.random.permutation(order_key, OWNERS)
    positions = jnp.arange(FRAMES)
    utterance = jnp.sum((positions[:, None] >= starts[None, :]).astype(jnp.int32), axis=1) - 1
    owners_of = assign[utterance].astype(jnp.int32)
    offsets = (positions - starts[utterance]).astype(jnp.int32)
    owner_lengths = jnp.zeros((OWNERS,), jnp.int32).at[assign].set(lengths.astype(jnp.int32))
    return (owners_of, offsets, owner_lengths)


def draw_frame_holder(key, part):
    return utterance_layout(key)[0]


def draw_frame_position(key, part):
    return utterance_layout(key)[1]


def draw_holder_utterance_length(key, part):
    return utterance_layout(key)[2]


def draw_hidden(key, part):
    col_key, row_key, entry_key = jax.random.split(jax.random.fold_in(key, 3), 3)
    column_scale = jnp.exp(jax.random.uniform(col_key, (D,), minval=0.0, maxval=math.log(10.0)))
    row_scale = jnp.exp(jax.random.uniform(row_key, (2, FRAMES, 1), minval=math.log(0.5), maxval=math.log(2.0)))
    entries = jax.random.normal(entry_key, (2, FRAMES, D))
    return (0.3 * entries * column_scale * row_scale).astype(jnp.bfloat16)


def levels(stream_key, extent, cuts, smallest, high):
    def one(dim, blocks):
        heights = jax.random.uniform(jax.random.fold_in(jax.random.fold_in(stream_key, 6), dim), (blocks,), jnp.float32, smallest / len(cuts), high / len(cuts))
        return jnp.repeat(jnp.exp(heights), extent[dim] // blocks).reshape((-1,) + (1,) * (len(extent) - dim - 1))

    factor_of = one(*cuts[0])
    for cut in cuts[1:]:
        factor_of = factor_of * one(*cut)
    return factor_of


def gaussian(stream_key, extent, scale, bound, cuts=(), kind=jnp.bfloat16):
    array = scale * jax.random.normal(stream_key, extent, jnp.float32)
    if cuts:
        array = array * levels(stream_key, extent, cuts, -0.22, 0.18)
    return jnp.clip(array, -bound, bound).astype(kind)


def setup_inputs(seed: int = 0) -> dict:
    key_of = jax.random.split(jax.random.key(seed), 23)
    hidden = draw_hidden(jax.random.fold_in(key_of[22], 71), 0)
    noisy_mel_state = gaussian(key_of[1], (BINS, FRAMES), 1.0, 6.0, ((1, 16),), jnp.float32)
    modulation = gaussian(key_of[2], (5, D), 0.5, 3.0, (), jnp.float32)
    feedforward_in_weight = gaussian(key_of[3], (D, FF), D ** -0.5, 0.1875)
    feedforward_in_bias = gaussian(key_of[4], (FF,), 0.3, 1.75, (), jnp.float32)
    feedforward_out_weight = gaussian(key_of[5], (FF, D), FF ** -0.5, 0.125)
    feedforward_out_bias = gaussian(key_of[6], (D,), 0.3, 1.75, (), jnp.float32)
    mel_velocity_weight = gaussian(key_of[7], (D, BINS), D ** -0.5, 0.1875)
    mel_velocity_bias = gaussian(key_of[8], (BINS,), 0.5, 3.0, (), jnp.float32)
    input_conv_weight = gaussian(key_of[9], (KPRE * BINS, CH0), (KPRE * BINS) ** -0.5, 0.21875)
    input_conv_bias = gaussian(key_of[10], (CH0,), 0.3, 1.75, (), jnp.float32)
    transposed_conv_weight = gaussian(key_of[11], (KT * UPSAMPLED_CHANS, CH0), (2 * CH0) ** -0.5, 0.1875)
    transposed_conv_bias = gaussian(key_of[12], (UPSAMPLED_CHANS,), 0.3, 1.75, (), jnp.float32)
    snake_freq_first = jnp.clip(jnp.exp(jax.random.uniform(key_of[13], (UPSAMPLED_CHANS,), jnp.float32, math.log(0.5), math.log(3.0))), 0.5, 3.0)
    dilated_conv_weight = gaussian(key_of[14], (3 * UPSAMPLED_CHANS, UPSAMPLED_CHANS), (3 * UPSAMPLED_CHANS) ** -0.5, 0.21875)
    dilated_conv_bias = gaussian(key_of[15], (UPSAMPLED_CHANS,), 0.3, 1.75, (), jnp.float32)
    snake_freq_second = jnp.clip(jnp.exp(jax.random.uniform(key_of[16], (UPSAMPLED_CHANS,), jnp.float32, math.log(0.5), math.log(3.0))), 0.5, 3.0)
    second_conv_weight = gaussian(key_of[17], (3 * UPSAMPLED_CHANS, UPSAMPLED_CHANS), (3 * UPSAMPLED_CHANS) ** -0.5, 0.21875)
    second_conv_bias = gaussian(key_of[18], (UPSAMPLED_CHANS,), 0.3, 1.75, (), jnp.float32)
    frame_holder = draw_frame_holder(jax.random.fold_in(key_of[22], 71), 0)
    frame_position = draw_frame_position(jax.random.fold_in(key_of[22], 71), 0)
    holder_utterance_length = draw_holder_utterance_length(jax.random.fold_in(key_of[22], 71), 0)
    return dict(hidden=hidden, noisy_mel_state=noisy_mel_state, modulation=modulation, feedforward_in_weight=feedforward_in_weight, feedforward_in_bias=feedforward_in_bias, feedforward_out_weight=feedforward_out_weight, feedforward_out_bias=feedforward_out_bias, mel_velocity_weight=mel_velocity_weight, mel_velocity_bias=mel_velocity_bias, input_conv_weight=input_conv_weight, input_conv_bias=input_conv_bias, transposed_conv_weight=transposed_conv_weight, transposed_conv_bias=transposed_conv_bias, snake_freq_first=snake_freq_first, dilated_conv_weight=dilated_conv_weight, dilated_conv_bias=dilated_conv_bias, snake_freq_second=snake_freq_second, second_conv_weight=second_conv_weight, second_conv_bias=second_conv_bias, frame_holder=frame_holder, frame_position=frame_position, holder_utterance_length=holder_utterance_length)


GUIDE = 2.0

def layer_norm(row_block):
    row_mean = lax.optimization_barrier(jnp.mean(row_block, axis=-1, keepdims=True))
    centred = row_block - row_mean
    row_var = lax.optimization_barrier(jnp.mean(centred * centred, axis=-1, keepdims=True))
    return centred * lax.rsqrt(row_var + 1e-06)

def velocity(row_block, modulation, feedforward_in_weight, feedforward_in_bias, feedforward_out_weight, feedforward_out_bias, mel_velocity_weight, mel_velocity_bias):
    residual_in = row_block.astype(jnp.float32)
    normed = (layer_norm(residual_in) * (1.0 + modulation[1]) + modulation[0]).astype(jnp.bfloat16)
    inner_pre = jnp.dot(normed, feedforward_in_weight, preferred_element_type=jnp.float32) + feedforward_in_bias
    active = jax.nn.gelu(inner_pre, approximate=True).astype(jnp.bfloat16)
    back_proj = jnp.dot(active, feedforward_out_weight, preferred_element_type=jnp.float32) + feedforward_out_bias
    block_out = residual_in + modulation[2] * back_proj
    final_norm = (layer_norm(block_out) * (1.0 + modulation[4]) + modulation[3]).astype(jnp.bfloat16)
    speed = lax.dot_general(mel_velocity_weight, final_norm, (((0,), (1,)), ((), ())), preferred_element_type=jnp.float32)
    return speed + mel_velocity_bias[:, None]

def shifted(values, offset):
    pad_width = abs(offset)
    last_axis = values.ndim - 1
    pad_spec = [(0, 0)] * last_axis + [(pad_width, pad_width)]
    padded = jnp.pad(values, pad_spec)
    return lax.slice_in_dim(padded, pad_width + offset, pad_width + offset + values.shape[last_axis], axis=last_axis)

def snake(signal, alpha_vec):
    sine_part = jnp.sin(alpha_vec[:, None] * signal)
    return signal + sine_part * sine_part / alpha_vec[:, None]

def dilated_output(values, weight, bias_vec, spacing, keep_mask):
    stacked = jnp.concatenate([shifted(values, -spacing), values, shifted(values, spacing)], axis=0)
    conv_out = lax.dot_general(weight, stacked, (((0,), (0,)), ((), ())), preferred_element_type=jnp.float32)
    return jnp.where(keep_mask[None, :], conv_out + bias_vec[:, None], 0.0)

def vocoder_synthesize(holder_mel, utterance_frames_length, input_conv_weight, input_conv_bias, transposed_conv_weight, transposed_conv_bias, snake_freq_first, dilated_conv_weight, dilated_conv_bias, snake_freq_second, second_conv_weight, second_conv_bias):
    most_rows = holder_mel.shape[1]
    channels = transposed_conv_weight.shape[0] // KT
    frame_keep = jnp.arange(most_rows) < utterance_frames_length
    half_kernel = KPRE // 2
    tap_list = [shifted(holder_mel, tap_index - half_kernel) for tap_index in range(KPRE)]
    stacked = jnp.concatenate(tap_list, axis=0)
    pre_out = lax.dot_general(input_conv_weight, stacked, (((0,), (0,)), ((), ())), preferred_element_type=jnp.float32)
    pre_out = jnp.where(frame_keep[None, :], pre_out + input_conv_bias[:, None], 0.0).astype(jnp.bfloat16)
    phases = jnp.dot(transposed_conv_weight, pre_out, preferred_element_type=jnp.float32).reshape(KT, channels, most_rows)
    pad_up = UP // 2
    direct = phases[pad_up:pad_up + UP]
    early_part = shifted(phases[UP + pad_up:], -1)
    late_part = shifted(phases[:UP - pad_up], 1)
    phase_sum = direct + jnp.concatenate([early_part, late_part], axis=0)
    woven_out = jnp.transpose(phase_sum, (1, 2, 0)).reshape(channels, most_rows * UP) + transposed_conv_bias[:, None]
    sample_keep_mask = jnp.arange(most_rows * UP) < utterance_frames_length * UP
    upsampled = jnp.where(sample_keep_mask[None, :], woven_out, 0.0).astype(jnp.bfloat16)
    first_snake_output = snake(upsampled.astype(jnp.float32), snake_freq_first).astype(jnp.bfloat16)
    inner_convolved = dilated_output(first_snake_output, dilated_conv_weight, dilated_conv_bias, DILATION_RATE, sample_keep_mask)
    second_act = snake(inner_convolved, snake_freq_second).astype(jnp.bfloat16)
    outer_conv = dilated_output(second_act, second_conv_weight, second_conv_bias, 1, sample_keep_mask)
    return (upsampled.astype(jnp.float32) + outer_conv).astype(jnp.bfloat16)

def reference(hidden, noisy_mel_state, modulation, feedforward_in_weight, feedforward_in_bias, feedforward_out_weight, feedforward_out_bias, mel_velocity_weight, mel_velocity_bias, input_conv_weight, input_conv_bias, transposed_conv_weight, transposed_conv_bias, snake_freq_first, dilated_conv_weight, dilated_conv_bias, snake_freq_second, second_conv_weight, second_conv_bias, frame_holder, frame_position, holder_utterance_length):
    step_size = math.cos(0.5 * math.pi * (NFE - 1) / NFE)
    block_count = 2 * FRAMES // F_DEV
    grouped = hidden.reshape(block_count, F_DEV, D)

    def one_block(row_block):
        return velocity(row_block, modulation, feedforward_in_weight, feedforward_in_bias, feedforward_out_weight, feedforward_out_bias, mel_velocity_weight, mel_velocity_bias)
    speeds = lax.map(one_block, grouped)
    speeds = speeds.reshape(2, N_SEQ, BINS, F_DEV).transpose(0, 2, 1, 3).reshape(2, BINS, FRAMES)
    guided = (1.0 + GUIDE) * speeds[0] - GUIDE * speeds[1]
    refined = (noisy_mel_state + step_size * guided).astype(jnp.bfloat16)
    flat_slot = frame_holder.astype(jnp.int32) * MOST + frame_position.astype(jnp.int32)
    placed = jnp.zeros((BINS, OWNERS * MOST), jnp.bfloat16).at[:, flat_slot].set(refined)
    owned_all = placed.reshape(BINS, OWNERS, MOST).transpose(1, 0, 2)

    def one_owner(paired_element):
        return vocoder_synthesize(paired_element[0], paired_element[1], input_conv_weight, input_conv_bias, transposed_conv_weight, transposed_conv_bias, snake_freq_first, dilated_conv_weight, dilated_conv_bias, snake_freq_second, second_conv_weight, second_conv_bias)
    return lax.map(one_owner, (owned_all, holder_utterance_length))
```

```python
import math

import jax
import jax.numpy as jnp
from jax import lax
from jax.experimental import pallas as pl
from jax.experimental.pallas import tpu as pltpu
from jax.sharding import PartitionSpec as P

UP = 8
KT = 16
KPRE = 7
DILATION_RATE = 3
NFE = 16

GUIDE = 2.0
LANES = 128
PAD = 16
CHUNK = 256
GROUP = 32
SERIES = tuple(
    factor * math.pi ** (2 * power + 2)
    for power, factor in enumerate(
        (
            0.9999998490771234,
            -0.3333321377542852,
            0.04444128701478595,
            -0.0031707593706167504,
            0.00013871416537404423,
            -3.540445572482011e-06,
        )
    )
)


def partner(block, axis, distance):
    count = lax.axis_size(axis)
    route = []
    for low in range(count):
        high = low | 1 << distance
        if high != low and high < count:
            route += [(low, high), (high, low)]
    return lax.ppermute(block, axis, route)


def layer_norm(row_block):
    row_mean = jnp.mean(row_block, axis=-1, keepdims=True)
    centred = row_block - row_mean
    row_var = jnp.mean(centred * centred, axis=-1, keepdims=True)
    return centred * lax.rsqrt(row_var + 1e-06)


def velocity(
    row_block,
    modulation,
    feedforward_in_weight,
    feedforward_in_bias,
    feedforward_out_weight,
    feedforward_out_bias,
    mel_velocity_weight,
    mel_velocity_bias,
):
    residual_in = row_block.astype(jnp.float32)
    normed = (layer_norm(residual_in) * (1.0 + modulation[1]) + modulation[0]).astype(jnp.bfloat16)
    inner_pre = (
        jnp.dot(normed, feedforward_in_weight, preferred_element_type=jnp.float32)
        + feedforward_in_bias
    )
    active = jax.nn.gelu(inner_pre, approximate=True).astype(jnp.bfloat16)
    back_proj = (
        jnp.dot(active, feedforward_out_weight, preferred_element_type=jnp.float32)
        + feedforward_out_bias
    )
    block_out = residual_in + modulation[2] * back_proj
    final_norm = (layer_norm(block_out) * (1.0 + modulation[4]) + modulation[3]).astype(
        jnp.bfloat16
    )
    speed = jnp.dot(final_norm, mel_velocity_weight, preferred_element_type=jnp.float32)
    return speed + mel_velocity_bias


def snake(signal, turns, inverse):
    spin = signal * turns
    spin = spin - jnp.round(spin)
    square = spin * spin
    series = SERIES[-1]
    for factor in SERIES[-2::-1]:
        series = series * square + factor
    return signal + (series * square) * inverse


def product(left, right, left_dim, right_dim):
    return lax.dot_general(
        left, right, (((left_dim,), (right_dim,)), ((), ())), preferred_element_type=jnp.float32
    )


def vocoder_kernel(
    length_ref,
    mel_ref,
    pre_w_ref,
    pre_b_ref,
    up_w_ref,
    up_b_ref,
    turns_first_ref,
    inverse_first_ref,
    dil_w_ref,
    dil_b_ref,
    turns_second_ref,
    inverse_second_ref,
    second_w_ref,
    second_b_ref,
    weave_ref,
    out_ref,
    mel_pad,
    pre_pad,
    up_keep,
    act_first,
    act_second,
):
    rows = mel_ref.shape[0]
    channels = out_ref.shape[0]
    chunk = math.gcd(rows, CHUNK)
    length = length_ref[0]
    lanes = mel_ref.shape[1]
    bf16 = jnp.bfloat16

    mel_pad[pl.ds(0, PAD)] = jnp.zeros((PAD, lanes), jnp.float32)
    mel_pad[pl.ds(PAD + rows, PAD)] = jnp.zeros((PAD, lanes), jnp.float32)
    skip = length_ref[1]
    rolled = pltpu.roll(mel_ref[...].astype(jnp.float32), lax.rem(rows - skip, rows), 0)
    inside = lax.broadcasted_iota(jnp.int32, (rows, 1), 0) < length
    mel_pad[pl.ds(PAD, rows)] = jnp.where(inside, rolled, 0.0)
    edge = jnp.zeros((PAD, pre_pad.shape[1]), bf16)
    pre_pad[pl.ds(0, PAD)] = edge
    pre_pad[pl.ds(PAD + rows, PAD)] = edge
    edge = jnp.zeros((UP, PAD, channels), bf16)
    for act in (act_first, act_second):
        act[:, pl.ds(0, PAD)] = edge
        act[:, pl.ds(PAD + rows, PAD)] = edge

    def keep_of(start):
        return start + lax.broadcasted_iota(jnp.int32, (chunk, 1), 0) < length

    def moved(window, offset):
        size = window.shape[0]
        wide = window.astype(jnp.float32)
        return pltpu.roll(wide, size - PAD - offset, 0)[:chunk]

    @pl.loop(0, rows // chunk)
    def _(step):
        start = pl.multiple_of(step * chunk, chunk)
        window = mel_pad[pl.ds(start, chunk + 2 * PAD)]
        stacked = jnp.concatenate(
            [moved(window, k - KPRE // 2).astype(bf16) for k in range(KPRE)], axis=1
        )
        pre = product(stacked, pre_w_ref[...], 1, 0) + pre_b_ref[...]
        pre = jnp.where(keep_of(start), pre, 0.0).astype(bf16)
        pre_pad[pl.ds(PAD + start, chunk)] = pre

    half = UP // 2

    @pl.loop(0, rows // chunk)
    def _(step):
        start = pl.multiple_of(step * chunk, chunk)
        keep = keep_of(start)
        window = pre_pad[pl.ds(start, chunk + 2 * PAD)]
        here = window[PAD : PAD + chunk]
        before = moved(window, -1).astype(bf16)
        after = moved(window, 1).astype(bf16)
        for phase in range(UP):
            tap = phase + half
            other = tap + UP if phase < half else tap - UP
            side = before if phase < half else after
            value = product(here, up_w_ref[pl.ds(tap * channels, channels)], 1, 1)
            value = value + product(side, up_w_ref[pl.ds(other * channels, channels)], 1, 1)
            value = jnp.where(keep, value + up_b_ref[...], 0.0).astype(bf16)
            up_keep[phase, pl.ds(start, chunk)] = value
            first = snake(value.astype(jnp.float32), turns_first_ref[...], inverse_first_ref[...])
            act_first[phase, pl.ds(PAD + start, chunk)] = first.astype(bf16)

    def tap_of(act, start, phase):
        frame, inner = phase // UP, phase % UP
        if frame == 0:
            return act[inner, pl.ds(PAD + start, chunk)]
        return moved(act[inner, pl.ds(start, chunk + 2 * PAD)], frame).astype(bf16)

    def conv_of(act, start, phase, spacing, weight_ref):
        stacked = jnp.concatenate(
            [tap_of(act, start, phase + k * spacing) for k in (-1, 0, 1)], axis=1
        )
        return product(stacked, weight_ref[...], 1, 0)

    @pl.loop(0, rows // chunk)
    def _(step):
        start = pl.multiple_of(step * chunk, chunk)
        keep = keep_of(start)
        for phase in range(UP):
            inner = conv_of(act_first, start, phase, DILATION_RATE, dil_w_ref)
            inner = jnp.where(keep, inner + dil_b_ref[...], 0.0)
            second = snake(inner, turns_second_ref[...], inverse_second_ref[...])
            act_second[phase, pl.ds(PAD + start, chunk)] = second.astype(bf16)

    @pl.loop(0, rows // chunk)
    def _(step):
        start = pl.multiple_of(step * chunk, chunk)
        keep = keep_of(start)
        waves = []
        for phase in range(UP):
            outer = conv_of(act_second, start, phase, 1, second_w_ref)
            outer = jnp.where(keep, outer + second_b_ref[...], 0.0)
            kept = up_keep[phase, pl.ds(start, chunk)].astype(jnp.float32)
            waves.append((kept + outer).astype(bf16))
        for group in range(chunk // GROUP):
            picked = jnp.concatenate(
                [wave[group * GROUP : (group + 1) * GROUP] for wave in waves], axis=0
            )
            woven = product(picked, weave_ref[...], 0, 0).astype(bf16)
            width = UP * GROUP
            column = pl.multiple_of(start * UP + group * width, width)
            out_ref[:, pl.ds(column, width)] = woven


def vocoder_synthesize(
    holder_mel,
    utterance_frames_length,
    input_conv_weight,
    input_conv_bias,
    transposed_conv_weight,
    transposed_conv_bias,
    snake_freq_first,
    dilated_conv_weight,
    dilated_conv_bias,
    snake_freq_second,
    second_conv_weight,
    second_conv_bias,
):
    rows, lanes = holder_mel.shape
    channels = transposed_conv_weight.shape[0] // KT
    hidden_channels = input_conv_weight.shape[1]
    bins = input_conv_weight.shape[0] // KPRE
    pre_weight = input_conv_weight.reshape(KPRE, bins, hidden_channels)
    pre_weight = jnp.pad(pre_weight, ((0, 0), (0, lanes - bins), (0, 0)))
    pre_weight = pre_weight.reshape(KPRE * lanes, hidden_channels)
    width = UP * GROUP
    source = jnp.arange(width)[:, None]
    weave = (source % GROUP) * UP + source // GROUP == jnp.arange(width)[None, :]
    vmem = pl.BlockSpec(memory_space=pltpu.VMEM)
    return pl.pallas_call(
        vocoder_kernel,
        out_shape=jax.ShapeDtypeStruct((channels, rows * UP), jnp.bfloat16),
        in_specs=[pl.BlockSpec(memory_space=pltpu.SMEM)] + [vmem] * 14,
        out_specs=vmem,
        scratch_shapes=[
            pltpu.VMEM((rows + 2 * PAD, lanes), jnp.float32),
            pltpu.VMEM((rows + 2 * PAD, hidden_channels), jnp.bfloat16),
            pltpu.VMEM((UP, rows, channels), jnp.bfloat16),
            pltpu.VMEM((UP, rows + 2 * PAD, channels), jnp.bfloat16),
            pltpu.VMEM((UP, rows + 2 * PAD, channels), jnp.bfloat16),
        ],
        compiler_params=pltpu.CompilerParams(vmem_limit_bytes=40 * 1024 * 1024),
        cost_estimate=pl.CostEstimate(
            flops=2 * rows * (700 * 512 + 16 * 256 * 512 + 48 * 256 * 256),
            bytes_accessed=10_000_000,
            transcendentals=0,
        ),
        name="vocoder",
    )(
        utterance_frames_length,
        holder_mel,
        pre_weight,
        input_conv_bias[None],
        transposed_conv_weight,
        transposed_conv_bias[None],
        (snake_freq_first / math.pi)[None],
        (1.0 / snake_freq_first)[None],
        dilated_conv_weight,
        dilated_conv_bias[None],
        (snake_freq_second / math.pi)[None],
        (1.0 / snake_freq_second)[None],
        second_conv_weight,
        second_conv_bias[None],
        weave.astype(jnp.bfloat16),
    )


def begins(frame_holder, frame_position, holder_utterance_length):
    frame_count = frame_holder.shape[0]
    owners = jnp.arange(holder_utterance_length.shape[0], dtype=jnp.int32)
    frame = lax.axis_index("seq") * frame_count + jnp.arange(frame_count, dtype=jnp.int32)
    opens = (frame_holder[:, None] == owners[None, :]) & (frame_position == 0)[:, None]
    found = jnp.sum(jnp.where(opens, frame[:, None], 0), axis=0)
    return lax.psum(found.astype(jnp.float32), "seq").astype(jnp.int32)


def local(
    hidden,
    noisy_mel_state,
    modulation,
    feedforward_in_weight,
    feedforward_in_bias,
    feedforward_out_weight,
    feedforward_out_bias,
    mel_velocity_weight,
    mel_velocity_bias,
    input_conv_weight,
    input_conv_bias,
    transposed_conv_weight,
    transposed_conv_bias,
    snake_freq_first,
    dilated_conv_weight,
    dilated_conv_bias,
    snake_freq_second,
    second_conv_weight,
    second_conv_bias,
    frame_holder,
    frame_position,
    holder_utterance_length,
):
    step_size = math.cos(0.5 * math.pi * (NFE - 1) / NFE)
    own_velocity = velocity(
        hidden[0],
        modulation,
        feedforward_in_weight,
        feedforward_in_bias,
        feedforward_out_weight,
        feedforward_out_bias,
        mel_velocity_weight,
        mel_velocity_bias,
    )
    frame_count, mel_bins = own_velocity.shape
    half_rows = frame_count // 2
    branch_side = lax.axis_index("branch")
    own_half = lax.dynamic_slice_in_dim(own_velocity, branch_side * half_rows, half_rows, 0)
    other_half = lax.dynamic_slice_in_dim(own_velocity, (1 - branch_side) * half_rows, half_rows, 0)
    peer_half = partner(other_half, "branch", 0)
    conditional = jnp.where(branch_side == 0, own_half, peer_half)
    unconditional = jnp.where(branch_side == 0, peer_half, own_half)
    guided = (1.0 + GUIDE) * conditional - GUIDE * unconditional
    noisy_half = lax.dynamic_slice_in_dim(noisy_mel_state, branch_side * half_rows, half_rows, 1)
    refined = (noisy_half.T + step_size * guided).astype(jnp.bfloat16)
    refined = jnp.pad(refined, ((0, 0), (0, -mel_bins % LANES)))

    self_owner = lax.axis_index(("branch", "seq"))
    utterance_frames_length = holder_utterance_length[self_owner]
    begin = begins(frame_holder, frame_position, holder_utterance_length)[self_owner]
    frames = lax.all_gather(refined, ("seq", "branch"), axis=0, tiled=True)
    first = jnp.minimum(begin, frames.shape[0] - frame_count)
    holder_mel = lax.dynamic_slice_in_dim(frames, first, frame_count, 0)
    utterance_frames_length = jnp.stack([utterance_frames_length, begin - first])
    wave = vocoder_synthesize(
        holder_mel,
        utterance_frames_length,
        input_conv_weight,
        input_conv_bias,
        transposed_conv_weight,
        transposed_conv_bias,
        snake_freq_first,
        dilated_conv_weight,
        dilated_conv_bias,
        snake_freq_second,
        second_conv_weight,
        second_conv_bias,
    )
    return wave[None]


def solution(mesh):
    return jax.shard_map(
        local,
        mesh=mesh,
        in_specs=(
            P("branch", "seq", None),
            P(None, "seq"),
            P(),
            P(),
            P(),
            P(),
            P(),
            P(),
            P(),
            P(),
            P(),
            P(),
            P(),
            P(),
            P(),
            P(),
            P(),
            P(),
            P(),
            P("seq"),
            P("seq"),
            P(),
        ),
        out_specs=P(("branch", "seq"), None, None),
        check_vma=False,
    )
```

```python
import functools
import math

import jax
import jax.numpy as jnp
from jax import lax
from jax.experimental import pallas as pl
from jax.experimental.pallas import tpu as pltpu
from jax.sharding import PartitionSpec as P

UP = 8
KT = 16
KPRE = 7
DILATION_RATE = 3
NFE = 16

GUIDE = 2.0
LANES = 128
PAD = 16
CHUNK = 256
GROUP = 32
SERIES = tuple(
    factor * math.pi ** (2 * power + 2)
    for power, factor in enumerate(
        (
            0.9999998490771234,
            -0.3333321377542852,
            0.04444128701478595,
            -0.0031707593706167504,
            0.00013871416537404423,
            -3.540445572482011e-06,
        )
    )
)


def partner(block, axis, distance):
    count = lax.axis_size(axis)
    route = []
    for low in range(count):
        high = low | 1 << distance
        if high != low and high < count:
            route += [(low, high), (high, low)]
    return lax.ppermute(block, axis, route)


def layer_norm(row_block):
    row_mean = jnp.mean(row_block, axis=-1, keepdims=True)
    centred = row_block - row_mean
    row_var = jnp.mean(centred * centred, axis=-1, keepdims=True)
    return centred * lax.rsqrt(row_var + 1e-06)


def velocity(
    row_block,
    modulation,
    feedforward_in_weight,
    feedforward_in_bias,
    feedforward_out_weight,
    feedforward_out_bias,
    mel_velocity_weight,
    mel_velocity_bias,
):
    residual_in = row_block.astype(jnp.float32)
    normed = (layer_norm(residual_in) * (1.0 + modulation[1]) + modulation[0]).astype(jnp.bfloat16)
    inner_pre = (
        jnp.dot(normed, feedforward_in_weight, preferred_element_type=jnp.float32)
        + feedforward_in_bias
    )
    active = jax.nn.gelu(inner_pre, approximate=True).astype(jnp.bfloat16)
    back_proj = (
        jnp.dot(active, feedforward_out_weight, preferred_element_type=jnp.float32)
        + feedforward_out_bias
    )
    block_out = residual_in + modulation[2] * back_proj
    final_norm = (layer_norm(block_out) * (1.0 + modulation[4]) + modulation[3]).astype(
        jnp.bfloat16
    )
    speed = jnp.dot(final_norm, mel_velocity_weight, preferred_element_type=jnp.float32)
    return speed + mel_velocity_bias


def snake(signal, turns, inverse):
    spin = signal * turns
    spin = spin - jnp.round(spin)
    square = spin * spin
    series = SERIES[-1]
    for factor in SERIES[-2::-1]:
        series = series * square + factor
    return signal + (series * square) * inverse


def product(left, right, left_dim, right_dim):
    return lax.dot_general(
        left, right, (((left_dim,), (right_dim,)), ((), ())), preferred_element_type=jnp.float32
    )


def vocoder_kernel(
    length_ref,
    mel_ref,
    pre_w_ref,
    pre_b_ref,
    up_w_ref,
    up_b_ref,
    turns_first_ref,
    inverse_first_ref,
    dil_w_ref,
    dil_b_ref,
    turns_second_ref,
    inverse_second_ref,
    second_w_ref,
    second_b_ref,
    weave_ref,
    out_ref,
    mel_pad,
    pre_pad,
    up_keep,
    act_first,
    act_second,
):
    rows = mel_ref.shape[0]
    channels = out_ref.shape[0]
    chunk = math.gcd(rows, CHUNK)
    length = length_ref[0]
    lanes = mel_ref.shape[1]
    bf16 = jnp.bfloat16

    mel_pad[pl.ds(0, PAD)] = jnp.zeros((PAD, lanes), jnp.float32)
    mel_pad[pl.ds(PAD + rows, PAD)] = jnp.zeros((PAD, lanes), jnp.float32)
    skip = length_ref[1]
    rolled = pltpu.roll(mel_ref[...].astype(jnp.float32), lax.rem(rows - skip, rows), 0)
    inside = lax.broadcasted_iota(jnp.int32, (rows, 1), 0) < length
    mel_pad[pl.ds(PAD, rows)] = jnp.where(inside, rolled, 0.0)
    edge = jnp.zeros((PAD, pre_pad.shape[1]), bf16)
    pre_pad[pl.ds(0, PAD)] = edge
    pre_pad[pl.ds(PAD + rows, PAD)] = edge
    edge = jnp.zeros((UP, PAD, channels), bf16)
    for act in (act_first, act_second):
        act[:, pl.ds(0, PAD)] = edge
        act[:, pl.ds(PAD + rows, PAD)] = edge

    def keep_of(start):
        return start + lax.broadcasted_iota(jnp.int32, (chunk, 1), 0) < length

    def moved(window, offset):
        size = window.shape[0]
        wide = window.astype(jnp.float32)
        return pltpu.roll(wide, size - PAD - offset, 0)[:chunk]

    @pl.loop(0, rows // chunk)
    def _(step):
        start = pl.multiple_of(step * chunk, chunk)
        window = mel_pad[pl.ds(start, chunk + 2 * PAD)]
        stacked = jnp.concatenate(
            [moved(window, k - KPRE // 2).astype(bf16) for k in range(KPRE)], axis=1
        )
        pre = product(stacked, pre_w_ref[...], 1, 0) + pre_b_ref[...]
        pre = jnp.where(keep_of(start), pre, 0.0).astype(bf16)
        pre_pad[pl.ds(PAD + start, chunk)] = pre

    half = UP // 2

    @pl.loop(0, rows // chunk)
    def _(step):
        start = pl.multiple_of(step * chunk, chunk)
        keep = keep_of(start)
        window = pre_pad[pl.ds(start, chunk + 2 * PAD)]
        here = window[PAD : PAD + chunk]
        before = moved(window, -1).astype(bf16)
        after = moved(window, 1).astype(bf16)
        for phase in range(UP):
            tap = phase + half
            other = tap + UP if phase < half else tap - UP
            side = before if phase < half else after
            value = product(here, up_w_ref[pl.ds(tap * channels, channels)], 1, 1)
            value = value + product(side, up_w_ref[pl.ds(other * channels, channels)], 1, 1)
            value = jnp.where(keep, value + up_b_ref[...], 0.0).astype(bf16)
            up_keep[phase, pl.ds(start, chunk)] = value
            first = snake(value.astype(jnp.float32), turns_first_ref[...], inverse_first_ref[...])
            act_first[phase, pl.ds(PAD + start, chunk)] = first.astype(bf16)

    def tap_of(act, start, phase):
        frame, inner = phase // UP, phase % UP
        if frame == 0:
            return act[inner, pl.ds(PAD + start, chunk)]
        return moved(act[inner, pl.ds(start, chunk + 2 * PAD)], frame).astype(bf16)

    def conv_of(act, start, phase, spacing, weight_ref):
        stacked = jnp.concatenate(
            [tap_of(act, start, phase + k * spacing) for k in (-1, 0, 1)], axis=1
        )
        return product(stacked, weight_ref[...], 1, 0)

    @pl.loop(0, rows // chunk)
    def _(step):
        start = pl.multiple_of(step * chunk, chunk)
        keep = keep_of(start)
        for phase in range(UP):
            inner = conv_of(act_first, start, phase, DILATION_RATE, dil_w_ref)
            inner = jnp.where(keep, inner + dil_b_ref[...], 0.0)
            second = snake(inner, turns_second_ref[...], inverse_second_ref[...])
            act_second[phase, pl.ds(PAD + start, chunk)] = second.astype(bf16)

    @pl.loop(0, rows // chunk)
    def _(step):
        start = pl.multiple_of(step * chunk, chunk)
        keep = keep_of(start)
        waves = []
        for phase in range(UP):
            outer = conv_of(act_second, start, phase, 1, second_w_ref)
            outer = jnp.where(keep, outer + second_b_ref[...], 0.0)
            kept = up_keep[phase, pl.ds(start, chunk)].astype(jnp.float32)
            waves.append((kept + outer).astype(bf16))
        for group in range(chunk // GROUP):
            picked = jnp.concatenate(
                [wave[group * GROUP : (group + 1) * GROUP] for wave in waves], axis=0
            )
            woven = product(picked, weave_ref[...], 0, 0).astype(bf16)
            width = UP * GROUP
            column = pl.multiple_of(start * UP + group * width, width)
            out_ref[:, pl.ds(column, width)] = woven


def vocoder_synthesize(
    holder_mel,
    utterance_frames_length,
    input_conv_weight,
    input_conv_bias,
    transposed_conv_weight,
    transposed_conv_bias,
    snake_freq_first,
    dilated_conv_weight,
    dilated_conv_bias,
    snake_freq_second,
    second_conv_weight,
    second_conv_bias,
):
    rows, lanes = holder_mel.shape
    channels = transposed_conv_weight.shape[0] // KT
    hidden_channels = input_conv_weight.shape[1]
    bins = input_conv_weight.shape[0] // KPRE
    pre_weight = input_conv_weight.reshape(KPRE, bins, hidden_channels)
    pre_weight = jnp.pad(pre_weight, ((0, 0), (0, lanes - bins), (0, 0)))
    pre_weight = pre_weight.reshape(KPRE * lanes, hidden_channels)
    width = UP * GROUP
    source = jnp.arange(width)[:, None]
    weave = (source % GROUP) * UP + source // GROUP == jnp.arange(width)[None, :]
    vmem = pl.BlockSpec(memory_space=pltpu.VMEM)
    return pl.pallas_call(
        vocoder_kernel,
        out_shape=jax.ShapeDtypeStruct((channels, rows * UP), jnp.bfloat16),
        in_specs=[pl.BlockSpec(memory_space=pltpu.SMEM)] + [vmem] * 14,
        out_specs=vmem,
        scratch_shapes=[
            pltpu.VMEM((rows + 2 * PAD, lanes), jnp.float32),
            pltpu.VMEM((rows + 2 * PAD, hidden_channels), jnp.bfloat16),
            pltpu.VMEM((UP, rows, channels), jnp.bfloat16),
            pltpu.VMEM((UP, rows + 2 * PAD, channels), jnp.bfloat16),
            pltpu.VMEM((UP, rows + 2 * PAD, channels), jnp.bfloat16),
        ],
        compiler_params=pltpu.CompilerParams(vmem_limit_bytes=40 * 1024 * 1024),
        cost_estimate=pl.CostEstimate(
            flops=2 * rows * (700 * 512 + 16 * 256 * 512 + 48 * 256 * 256),
            bytes_accessed=10_000_000,
            transcendentals=0,
        ),
        name="vocoder",
    )(
        utterance_frames_length,
        holder_mel,
        pre_weight,
        input_conv_bias[None],
        transposed_conv_weight,
        transposed_conv_bias[None],
        (snake_freq_first / math.pi)[None],
        (1.0 / snake_freq_first)[None],
        dilated_conv_weight,
        dilated_conv_bias[None],
        (snake_freq_second / math.pi)[None],
        (1.0 / snake_freq_second)[None],
        second_conv_weight,
        second_conv_bias[None],
        weave.astype(jnp.bfloat16),
    )


def opening_rows(holders, positions):
    rows = holders.shape[0]
    frame = jnp.arange(rows, dtype=jnp.int32)[:, None]
    opens = (holders[:, None] == jnp.arange(LANES, dtype=jnp.int32)) & (positions == 0)[:, None]
    any_open = jnp.sum(opens.astype(jnp.int32), axis=0)
    place = jnp.sum(jnp.where(opens, frame, 0), axis=0)
    tags = jnp.stack([any_open, place // LANES, place % LANES]).astype(jnp.bfloat16)
    return jnp.pad(tags, ((0, 13), (0, 0)))


def gather_kernel(lines, block_ref, out_ref, *sems):
    line_sem, x_sem, y_sem, fx_sem, fy_sem, core_sem = (sems[2 * i : 2 * i + 2] for i in range(6))
    branch = lax.axis_index("branch")
    seq = lax.axis_index("seq")
    line, y, x = seq // 4, lax.rem(seq, 4) // 2, lax.rem(seq, 2)
    rows = block_ref.shape[0]
    half = rows // 32 * 16

    def at(line_, y_, x_):
        return line_ * 4 + y_ * 2 + x_

    x_side, y_side = (branch, at(line, y, 1 - x)), (branch, at(line, 1 - y, x))
    core_side = (1 - branch, seq)
    along = [(branch, at(lax.rem(line + d, lines), y, x)) for d in range(lines)]

    barrier = pltpu.get_barrier_semaphore()
    partners = along[1:] + [x_side, y_side, core_side]
    for device in partners:
        pl.semaphore_signal(barrier, inc=1, device_id=device, device_id_type=pl.DeviceIdType.MESH)
    out_ref[seq * 2 + branch] = block_ref[...]
    pl.semaphore_wait(barrier, len(partners))

    started = []

    def send(index, start, size, device, pair, slot):
        piece = out_ref.at[index, pl.ds(start, size)]
        copy = pltpu.make_async_remote_copy(
            src_ref=piece,
            dst_ref=piece,
            send_sem=pair[0].at[slot],
            recv_sem=pair[1].at[slot],
            device_id=device,
            device_id_type=pl.DeviceIdType.MESH,
        )
        copy.start()
        started.append(copy)

    def arrived(index, start, size, device, pair, slot):
        piece = out_ref.at[index, pl.ds(start, size)]
        pltpu.make_async_remote_copy(
            src_ref=piece,
            dst_ref=piece,
            send_sem=pair[0].at[slot],
            recv_sem=pair[1].at[slot],
            device_id=device,
            device_id_type=pl.DeviceIdType.MESH,
        ).wait_recv()

    def block_of(d, y_, x_, side=branch):
        return at(lax.rem(line - d + lines, lines), y_, x_) * 2 + side

    def forward(d):
        over_x, over_y = block_of(d, y, 1 - x), block_of(d, 1 - y, x)
        arrived(over_x, 0, rows, x_side, x_sem, d)
        send(over_x, 0, half, y_side, fy_sem, d)
        arrived(over_y, 0, rows, y_side, y_sem, d)
        send(over_y, half, rows - half, x_side, fx_sem, d)
        send(over_x, 0, rows, core_side, core_sem, 4 * d + 1)
        send(over_y, 0, rows, core_side, core_sem, 4 * d + 2)

    def finish(d):
        corner = block_of(d, 1 - y, 1 - x)
        arrived(corner, 0, half, y_side, fy_sem, d)
        arrived(corner, half, rows - half, x_side, fx_sem, d)
        send(corner, 0, rows, core_side, core_sem, 4 * d + 3)

    for d in range(1, lines):
        send(seq * 2 + branch, 0, rows, along[d], line_sem, d)
    for d in range(lines):
        mine = block_of(d, y, x)
        if d:
            arrived(mine, 0, rows, along[d], line_sem, d)
        send(mine, 0, rows, x_side, x_sem, d)
        send(mine, 0, rows, y_side, y_sem, d)
        send(mine, 0, rows, core_side, core_sem, 4 * d)
        if d:
            forward(d - 1)
    forward(lines - 1)
    for d in range(lines):
        finish(d)
    for d in range(lines):
        for slot, (y_, x_) in enumerate(((y, x), (y, 1 - x), (1 - y, x), (1 - y, 1 - x))):
            arrived(block_of(d, y_, x_, 1 - branch), 0, rows, core_side, core_sem, 4 * d + slot)
    for copy in started:
        copy.wait_send()


def gather_blocks(block):
    seq_count = lax.axis_size("seq")
    lines = seq_count // 4
    dma = pltpu.SemaphoreType.DMA
    counts = (lines, lines, lines, lines, lines, 4 * lines)
    vmem = pl.BlockSpec(memory_space=pltpu.VMEM)
    return pl.pallas_call(
        functools.partial(gather_kernel, lines),
        out_shape=jax.ShapeDtypeStruct((2 * seq_count,) + block.shape, block.dtype),
        in_specs=[vmem],
        out_specs=vmem,
        scratch_shapes=[dma((count,)) for count in counts for _ in range(2)],
        compiler_params=pltpu.CompilerParams(
            collective_id=0, has_side_effects=True, vmem_limit_bytes=24 * 1024 * 1024
        ),
        name="gather_blocks",
    )(block)


def local(
    hidden,
    noisy_mel_state,
    modulation,
    feedforward_in_weight,
    feedforward_in_bias,
    feedforward_out_weight,
    feedforward_out_bias,
    mel_velocity_weight,
    mel_velocity_bias,
    input_conv_weight,
    input_conv_bias,
    transposed_conv_weight,
    transposed_conv_bias,
    snake_freq_first,
    dilated_conv_weight,
    dilated_conv_bias,
    snake_freq_second,
    second_conv_weight,
    second_conv_bias,
    frame_holder,
    frame_position,
    holder_utterance_length,
):
    step_size = math.cos(0.5 * math.pi * (NFE - 1) / NFE)
    own_velocity = velocity(
        hidden[0],
        modulation,
        feedforward_in_weight,
        feedforward_in_bias,
        feedforward_out_weight,
        feedforward_out_bias,
        mel_velocity_weight,
        mel_velocity_bias,
    )
    frame_count, mel_bins = own_velocity.shape
    half_rows = frame_count // 2
    branch_side = lax.axis_index("branch")
    own_half = lax.dynamic_slice_in_dim(own_velocity, branch_side * half_rows, half_rows, 0)
    other_half = lax.dynamic_slice_in_dim(own_velocity, (1 - branch_side) * half_rows, half_rows, 0)
    peer_half = partner(other_half, "branch", 0)
    conditional = jnp.where(branch_side == 0, own_half, peer_half)
    unconditional = jnp.where(branch_side == 0, peer_half, own_half)
    guided = (1.0 + GUIDE) * conditional - GUIDE * unconditional
    noisy_half = lax.dynamic_slice_in_dim(noisy_mel_state, branch_side * half_rows, half_rows, 1)
    refined = (noisy_half.T + step_size * guided).astype(jnp.bfloat16)
    refined = jnp.pad(refined, ((0, 0), (0, -mel_bins % LANES)))
    holders = lax.dynamic_slice_in_dim(frame_holder, branch_side * half_rows, half_rows, 0)
    positions = lax.dynamic_slice_in_dim(frame_position, branch_side * half_rows, half_rows, 0)
    block = jnp.concatenate([refined, opening_rows(holders, positions)], axis=0)

    self_owner = lax.axis_index(("branch", "seq"))
    length = holder_utterance_length[self_owner]
    blocks = gather_blocks(block)
    block_count = blocks.shape[0]
    tags = lax.dynamic_slice(blocks, (0, half_rows, self_owner), (block_count, 3, 1))
    tags = tags[:, :, 0].astype(jnp.float32)
    places = jnp.arange(block_count, dtype=jnp.float32) * half_rows
    begin = jnp.sum(tags[:, 0] * (places + LANES * tags[:, 1] + tags[:, 2])).astype(jnp.int32)
    low = jnp.minimum(begin // half_rows, block_count - 3)
    near = lax.dynamic_slice(blocks, (low, 0, 0), (3, half_rows, LANES)).reshape(-1, LANES)
    begin = begin - low * half_rows
    first = jnp.minimum(begin, near.shape[0] - frame_count)
    holder_mel = lax.dynamic_slice_in_dim(near, first, frame_count, 0)
    utterance_frames_length = jnp.stack([length, begin - first])
    wave = vocoder_synthesize(
        holder_mel,
        utterance_frames_length,
        input_conv_weight,
        input_conv_bias,
        transposed_conv_weight,
        transposed_conv_bias,
        snake_freq_first,
        dilated_conv_weight,
        dilated_conv_bias,
        snake_freq_second,
        second_conv_weight,
        second_conv_bias,
    )
    return wave[None]


def solution(mesh):
    return jax.shard_map(
        local,
        mesh=mesh,
        in_specs=(
            P("branch", "seq", None),
            P(None, "seq"),
            P(),
            P(),
            P(),
            P(),
            P(),
            P(),
            P(),
            P(),
            P(),
            P(),
            P(),
            P(),
            P(),
            P(),
            P(),
            P(),
            P(),
            P("seq"),
            P("seq"),
            P(),
        ),
        out_specs=P(("branch", "seq"), None, None),
        check_vma=False,
    )
```

```python
import functools
import math

import jax
import jax.numpy as jnp
from jax import lax
from jax.experimental import pallas as pl
from jax.experimental.pallas import tpu as pltpu
from jax.sharding import PartitionSpec as P

UP = 8
KT = 16
KPRE = 7
DILATION_RATE = 3
NFE = 16

GUIDE = 2.0
LANES = 128
PAD = 16
CHUNK = 256
GROUP = 32
SERIES = tuple(
    factor * math.pi ** (2 * power + 2)
    for power, factor in enumerate(
        (
            0.9999998490771234,
            -0.3333321377542852,
            0.04444128701478595,
            -0.0031707593706167504,
            0.00013871416537404423,
            -3.540445572482011e-06,
        )
    )
)


def partner(block, axis, distance):
    count = lax.axis_size(axis)
    route = []
    for low in range(count):
        high = low | 1 << distance
        if high != low and high < count:
            route += [(low, high), (high, low)]
    return lax.ppermute(block, axis, route)


def layer_norm(row_block):
    row_mean = jnp.mean(row_block, axis=-1, keepdims=True)
    centred = row_block - row_mean
    row_var = jnp.mean(centred * centred, axis=-1, keepdims=True)
    return centred * lax.rsqrt(row_var + 1e-06)


def velocity_kernel(
    rows_ref, mod_ref, in_w_ref, in_b_ref, out_w_ref, out_b_ref, mel_w_ref, mel_b_ref, out_ref,
    normed, total,
):
    step = pl.program_id(0)
    chunk = math.gcd(rows_ref.shape[0], CHUNK)
    pieces = [pl.ds(i * chunk, chunk) for i in range(rows_ref.shape[0] // chunk)]
    modulation = [mod_ref[i : i + 1] for i in range(5)]

    @pl.when(step == 0)
    def _():
        for piece in pieces:
            plain = layer_norm(rows_ref[piece].astype(jnp.float32))
            normed[piece] = (plain * (1.0 + modulation[1]) + modulation[0]).astype(jnp.bfloat16)
            total[piece] = jnp.zeros((chunk, total.shape[1]), jnp.float32)

    for piece in pieces:
        inner = product(normed[piece], in_w_ref[...], 1, 0) + in_b_ref[...]
        bend = inner * (math.sqrt(2.0 / math.pi) * (1.0 + 0.044715 * inner * inner))
        active = (0.5 * inner * (1.0 + jnp.tanh(bend))).astype(jnp.bfloat16)
        total[piece] += product(active, out_w_ref[...], 1, 0)

    @pl.when(step == pl.num_programs(0) - 1)
    def _():
        for piece in pieces:
            back = modulation[2] * (total[piece] + out_b_ref[...])
            plain = layer_norm(rows_ref[piece].astype(jnp.float32) + back)
            final = (plain * (1.0 + modulation[4]) + modulation[3]).astype(jnp.bfloat16)
            out_ref[piece] = product(final, mel_w_ref[...], 1, 0) + mel_b_ref[...]


def velocity(
    row_block,
    modulation,
    feedforward_in_weight,
    feedforward_in_bias,
    feedforward_out_weight,
    feedforward_out_bias,
    mel_velocity_weight,
    mel_velocity_bias,
):
    rows, width = row_block.shape
    inner = feedforward_in_weight.shape[1]
    part = math.gcd(inner, 512)
    spare = -mel_velocity_weight.shape[1] % LANES
    mel_weight = jnp.pad(mel_velocity_weight, ((0, 0), (0, spare)))
    mel_bias = jnp.pad(mel_velocity_bias, (0, spare))

    def whole(*shape):
        return pl.BlockSpec(shape, lambda i: (0,) * len(shape))

    lanes = mel_weight.shape[1]
    return pl.pallas_call(
        velocity_kernel,
        grid=(inner // part,),
        out_shape=jax.ShapeDtypeStruct((rows, lanes), jnp.float32),
        in_specs=[
            whole(rows, width),
            whole(5, width),
            pl.BlockSpec((width, part), lambda i: (0, i)),
            pl.BlockSpec((1, part), lambda i: (0, i)),
            pl.BlockSpec((part, width), lambda i: (i, 0)),
            whole(1, width),
            whole(width, lanes),
            whole(1, lanes),
        ],
        out_specs=whole(rows, lanes),
        scratch_shapes=[
            pltpu.VMEM((rows, width), jnp.bfloat16),
            pltpu.VMEM((rows, width), jnp.float32),
        ],
        compiler_params=pltpu.CompilerParams(vmem_limit_bytes=32 * 1024 * 1024),
        cost_estimate=pl.CostEstimate(
            flops=4 * rows * width * inner, bytes_accessed=11_000_000, transcendentals=rows * inner
        ),
        name="velocity",
    )(
        row_block,
        modulation,
        feedforward_in_weight,
        feedforward_in_bias[None],
        feedforward_out_weight,
        feedforward_out_bias[None],
        mel_weight,
        mel_bias[None],
    )


def snake(signal, turns, inverse):
    spin = signal * turns
    spin = spin - jnp.round(spin)
    square = spin * spin
    series = SERIES[-1]
    for factor in SERIES[-2::-1]:
        series = series * square + factor
    return signal + (series * square) * inverse


def product(left, right, left_dim, right_dim):
    return lax.dot_general(
        left, right, (((left_dim,), (right_dim,)), ((), ())), preferred_element_type=jnp.float32
    )


def vocoder_kernel(
    length_ref,
    mel_ref,
    pre_w_ref,
    pre_b_ref,
    up_w_ref,
    up_b_ref,
    turns_first_ref,
    inverse_first_ref,
    dil_w_ref,
    dil_b_ref,
    turns_second_ref,
    inverse_second_ref,
    second_w_ref,
    second_b_ref,
    weave_ref,
    out_ref,
    mel_pad,
    pre_pad,
    up_keep,
    act_first,
    act_second,
):
    rows = mel_ref.shape[0]
    channels = out_ref.shape[0]
    chunk = math.gcd(rows, CHUNK)
    length = length_ref[0]
    lanes = mel_ref.shape[1]
    bf16 = jnp.bfloat16

    mel_pad[pl.ds(0, PAD)] = jnp.zeros((PAD, lanes), jnp.float32)
    mel_pad[pl.ds(PAD + rows, PAD)] = jnp.zeros((PAD, lanes), jnp.float32)
    skip = length_ref[1]
    rolled = pltpu.roll(mel_ref[...].astype(jnp.float32), lax.rem(rows - skip, rows), 0)
    inside = lax.broadcasted_iota(jnp.int32, (rows, 1), 0) < length
    mel_pad[pl.ds(PAD, rows)] = jnp.where(inside, rolled, 0.0)
    edge = jnp.zeros((PAD, pre_pad.shape[1]), bf16)
    pre_pad[pl.ds(0, PAD)] = edge
    pre_pad[pl.ds(PAD + rows, PAD)] = edge
    edge = jnp.zeros((UP, PAD, channels), bf16)
    for act in (act_first, act_second):
        act[:, pl.ds(0, PAD)] = edge
        act[:, pl.ds(PAD + rows, PAD)] = edge

    def keep_of(start):
        return start + lax.broadcasted_iota(jnp.int32, (chunk, 1), 0) < length

    def moved(window, offset):
        size = window.shape[0]
        wide = window.astype(jnp.float32)
        return pltpu.roll(wide, size - PAD - offset, 0)[:chunk]

    @pl.loop(0, rows // chunk)
    def _(step):
        start = pl.multiple_of(step * chunk, chunk)
        window = mel_pad[pl.ds(start, chunk + 2 * PAD)]
        stacked = jnp.concatenate(
            [moved(window, k - KPRE // 2).astype(bf16) for k in range(KPRE)], axis=1
        )
        pre = product(stacked, pre_w_ref[...], 1, 0) + pre_b_ref[...]
        pre = jnp.where(keep_of(start), pre, 0.0).astype(bf16)
        pre_pad[pl.ds(PAD + start, chunk)] = pre

    half = UP // 2

    @pl.loop(0, rows // chunk)
    def _(step):
        start = pl.multiple_of(step * chunk, chunk)
        keep = keep_of(start)
        window = pre_pad[pl.ds(start, chunk + 2 * PAD)]
        here = window[PAD : PAD + chunk]
        before = moved(window, -1).astype(bf16)
        after = moved(window, 1).astype(bf16)
        for phase in range(UP):
            tap = phase + half
            other = tap + UP if phase < half else tap - UP
            side = before if phase < half else after
            value = product(here, up_w_ref[pl.ds(tap * channels, channels)], 1, 1)
            value = value + product(side, up_w_ref[pl.ds(other * channels, channels)], 1, 1)
            value = jnp.where(keep, value + up_b_ref[...], 0.0).astype(bf16)
            up_keep[phase, pl.ds(start, chunk)] = value
            first = snake(value.astype(jnp.float32), turns_first_ref[...], inverse_first_ref[...])
            act_first[phase, pl.ds(PAD + start, chunk)] = first.astype(bf16)

    def tap_of(act, start, phase):
        frame, inner = phase // UP, phase % UP
        if frame == 0:
            return act[inner, pl.ds(PAD + start, chunk)]
        return moved(act[inner, pl.ds(start, chunk + 2 * PAD)], frame).astype(bf16)

    def conv_of(act, start, phase, spacing, weight_ref):
        stacked = jnp.concatenate(
            [tap_of(act, start, phase + k * spacing) for k in (-1, 0, 1)], axis=1
        )
        return product(stacked, weight_ref[...], 1, 0)

    @pl.loop(0, rows // chunk)
    def _(step):
        start = pl.multiple_of(step * chunk, chunk)
        keep = keep_of(start)
        for phase in range(UP):
            inner = conv_of(act_first, start, phase, DILATION_RATE, dil_w_ref)
            inner = jnp.where(keep, inner + dil_b_ref[...], 0.0)
            second = snake(inner, turns_second_ref[...], inverse_second_ref[...])
            act_second[phase, pl.ds(PAD + start, chunk)] = second.astype(bf16)

    @pl.loop(0, rows // chunk)
    def _(step):
        start = pl.multiple_of(step * chunk, chunk)
        keep = keep_of(start)
        waves = []
        for phase in range(UP):
            outer = conv_of(act_second, start, phase, 1, second_w_ref)
            outer = jnp.where(keep, outer + second_b_ref[...], 0.0)
            kept = up_keep[phase, pl.ds(start, chunk)].astype(jnp.float32)
            waves.append((kept + outer).astype(bf16))
        for group in range(chunk // GROUP):
            picked = jnp.concatenate(
                [wave[group * GROUP : (group + 1) * GROUP] for wave in waves], axis=0
            )
            woven = product(picked, weave_ref[...], 0, 0).astype(bf16)
            width = UP * GROUP
            column = pl.multiple_of(start * UP + group * width, width)
            out_ref[:, pl.ds(column, width)] = woven


def vocoder_synthesize(
    holder_mel,
    utterance_frames_length,
    input_conv_weight,
    input_conv_bias,
    transposed_conv_weight,
    transposed_conv_bias,
    snake_freq_first,
    dilated_conv_weight,
    dilated_conv_bias,
    snake_freq_second,
    second_conv_weight,
    second_conv_bias,
):
    rows, lanes = holder_mel.shape
    channels = transposed_conv_weight.shape[0] // KT
    hidden_channels = input_conv_weight.shape[1]
    bins = input_conv_weight.shape[0] // KPRE
    pre_weight = input_conv_weight.reshape(KPRE, bins, hidden_channels)
    pre_weight = jnp.pad(pre_weight, ((0, 0), (0, lanes - bins), (0, 0)))
    pre_weight = pre_weight.reshape(KPRE * lanes, hidden_channels)
    width = UP * GROUP
    source = jnp.arange(width)[:, None]
    weave = (source % GROUP) * UP + source // GROUP == jnp.arange(width)[None, :]
    vmem = pl.BlockSpec(memory_space=pltpu.VMEM)
    return pl.pallas_call(
        vocoder_kernel,
        out_shape=jax.ShapeDtypeStruct((channels, rows * UP), jnp.bfloat16),
        in_specs=[pl.BlockSpec(memory_space=pltpu.SMEM)] + [vmem] * 14,
        out_specs=vmem,
        scratch_shapes=[
            pltpu.VMEM((rows + 2 * PAD, lanes), jnp.float32),
            pltpu.VMEM((rows + 2 * PAD, hidden_channels), jnp.bfloat16),
            pltpu.VMEM((UP, rows, channels), jnp.bfloat16),
            pltpu.VMEM((UP, rows + 2 * PAD, channels), jnp.bfloat16),
            pltpu.VMEM((UP, rows + 2 * PAD, channels), jnp.bfloat16),
        ],
        compiler_params=pltpu.CompilerParams(vmem_limit_bytes=40 * 1024 * 1024),
        cost_estimate=pl.CostEstimate(
            flops=2 * rows * (700 * 512 + 16 * 256 * 512 + 48 * 256 * 256),
            bytes_accessed=10_000_000,
            transcendentals=0,
        ),
        name="vocoder",
    )(
        utterance_frames_length,
        holder_mel,
        pre_weight,
        input_conv_bias[None],
        transposed_conv_weight,
        transposed_conv_bias[None],
        (snake_freq_first / math.pi)[None],
        (1.0 / snake_freq_first)[None],
        dilated_conv_weight,
        dilated_conv_bias[None],
        (snake_freq_second / math.pi)[None],
        (1.0 / snake_freq_second)[None],
        second_conv_weight,
        second_conv_bias[None],
        weave.astype(jnp.bfloat16),
    )


def opening_rows(holders, positions):
    rows = holders.shape[0]
    frame = jnp.arange(rows, dtype=jnp.int32)[:, None]
    opens = (holders[:, None] == jnp.arange(LANES, dtype=jnp.int32)) & (positions == 0)[:, None]
    any_open = jnp.sum(opens.astype(jnp.int32), axis=0)
    place = jnp.sum(jnp.where(opens, frame, 0), axis=0)
    tags = jnp.stack([any_open, place // LANES, place % LANES]).astype(jnp.bfloat16)
    return jnp.pad(tags, ((0, 13), (0, 0)))


def gather_kernel(lines, block_ref, out_ref, *sems):
    line_sem, x_sem, y_sem, fx_sem, fy_sem, core_sem = (sems[2 * i : 2 * i + 2] for i in range(6))
    branch = lax.axis_index("branch")
    seq = lax.axis_index("seq")
    line, y, x = seq // 4, lax.rem(seq, 4) // 2, lax.rem(seq, 2)
    rows = block_ref.shape[0]
    half = rows // 32 * 16

    def at(line_, y_, x_):
        return line_ * 4 + y_ * 2 + x_

    x_side, y_side = (branch, at(line, y, 1 - x)), (branch, at(line, 1 - y, x))
    core_side = (1 - branch, seq)
    along = [(branch, at(lax.rem(line + d, lines), y, x)) for d in range(lines)]

    barrier = pltpu.get_barrier_semaphore()
    partners = along[1:] + [x_side, y_side, core_side]
    for device in partners:
        pl.semaphore_signal(barrier, inc=1, device_id=device, device_id_type=pl.DeviceIdType.MESH)
    out_ref[seq * 2 + branch] = block_ref[...]
    pl.semaphore_wait(barrier, len(partners))

    started = []

    def send(index, start, size, device, pair, slot):
        piece = out_ref.at[index, pl.ds(start, size)]
        copy = pltpu.make_async_remote_copy(
            src_ref=piece,
            dst_ref=piece,
            send_sem=pair[0].at[slot],
            recv_sem=pair[1].at[slot],
            device_id=device,
            device_id_type=pl.DeviceIdType.MESH,
        )
        copy.start()
        started.append(copy)

    def arrived(index, start, size, device, pair, slot):
        piece = out_ref.at[index, pl.ds(start, size)]
        pltpu.make_async_remote_copy(
            src_ref=piece,
            dst_ref=piece,
            send_sem=pair[0].at[slot],
            recv_sem=pair[1].at[slot],
            device_id=device,
            device_id_type=pl.DeviceIdType.MESH,
        ).wait_recv()

    def block_of(d, y_, x_, side=branch):
        return at(lax.rem(line - d + lines, lines), y_, x_) * 2 + side

    def forward(d):
        over_x, over_y = block_of(d, y, 1 - x), block_of(d, 1 - y, x)
        arrived(over_x, 0, rows, x_side, x_sem, d)
        send(over_x, 0, half, y_side, fy_sem, d)
        arrived(over_y, 0, rows, y_side, y_sem, d)
        send(over_y, half, rows - half, x_side, fx_sem, d)
        send(over_x, 0, rows, core_side, core_sem, 4 * d + 1)
        send(over_y, 0, rows, core_side, core_sem, 4 * d + 2)

    def finish(d):
        corner = block_of(d, 1 - y, 1 - x)
        arrived(corner, 0, half, y_side, fy_sem, d)
        arrived(corner, half, rows - half, x_side, fx_sem, d)
        send(corner, 0, rows, core_side, core_sem, 4 * d + 3)

    for d in range(1, lines):
        send(seq * 2 + branch, 0, rows, along[d], line_sem, d)
    for d in range(lines):
        mine = block_of(d, y, x)
        if d:
            arrived(mine, 0, rows, along[d], line_sem, d)
        send(mine, 0, rows, x_side, x_sem, d)
        send(mine, 0, rows, y_side, y_sem, d)
        send(mine, 0, rows, core_side, core_sem, 4 * d)
        if d:
            forward(d - 1)
    forward(lines - 1)
    for d in range(lines):
        finish(d)
    for d in range(lines):
        for slot, (y_, x_) in enumerate(((y, x), (y, 1 - x), (1 - y, x), (1 - y, 1 - x))):
            arrived(block_of(d, y_, x_, 1 - branch), 0, rows, core_side, core_sem, 4 * d + slot)
    for copy in started:
        copy.wait_send()


def gather_blocks(block):
    seq_count = lax.axis_size("seq")
    lines = seq_count // 4
    dma = pltpu.SemaphoreType.DMA
    counts = (lines, lines, lines, lines, lines, 4 * lines)
    vmem = pl.BlockSpec(memory_space=pltpu.VMEM)
    return pl.pallas_call(
        functools.partial(gather_kernel, lines),
        out_shape=jax.ShapeDtypeStruct((2 * seq_count,) + block.shape, block.dtype),
        in_specs=[vmem],
        out_specs=vmem,
        scratch_shapes=[dma((count,)) for count in counts for _ in range(2)],
        compiler_params=pltpu.CompilerParams(
            collective_id=0, has_side_effects=True, vmem_limit_bytes=24 * 1024 * 1024
        ),
        name="gather_blocks",
    )(block)


def local(
    hidden,
    noisy_mel_state,
    modulation,
    feedforward_in_weight,
    feedforward_in_bias,
    feedforward_out_weight,
    feedforward_out_bias,
    mel_velocity_weight,
    mel_velocity_bias,
    input_conv_weight,
    input_conv_bias,
    transposed_conv_weight,
    transposed_conv_bias,
    snake_freq_first,
    dilated_conv_weight,
    dilated_conv_bias,
    snake_freq_second,
    second_conv_weight,
    second_conv_bias,
    frame_holder,
    frame_position,
    holder_utterance_length,
):
    step_size = math.cos(0.5 * math.pi * (NFE - 1) / NFE)
    own_velocity = velocity(
        hidden[0],
        modulation,
        feedforward_in_weight,
        feedforward_in_bias,
        feedforward_out_weight,
        feedforward_out_bias,
        mel_velocity_weight,
        mel_velocity_bias,
    )
    frame_count, lanes = own_velocity.shape
    half_rows = frame_count // 2
    branch_side = lax.axis_index("branch")
    own_half = lax.dynamic_slice_in_dim(own_velocity, branch_side * half_rows, half_rows, 0)
    other_half = lax.dynamic_slice_in_dim(own_velocity, (1 - branch_side) * half_rows, half_rows, 0)
    peer_half = partner(other_half, "branch", 0)
    conditional = jnp.where(branch_side == 0, own_half, peer_half)
    unconditional = jnp.where(branch_side == 0, peer_half, own_half)
    guided = (1.0 + GUIDE) * conditional - GUIDE * unconditional
    noisy_half = lax.dynamic_slice_in_dim(noisy_mel_state, branch_side * half_rows, half_rows, 1)
    noisy_half = jnp.pad(noisy_half, ((0, lanes - noisy_half.shape[0]), (0, 0)))
    refined = (noisy_half.T + step_size * guided).astype(jnp.bfloat16)
    holders = lax.dynamic_slice_in_dim(frame_holder, branch_side * half_rows, half_rows, 0)
    positions = lax.dynamic_slice_in_dim(frame_position, branch_side * half_rows, half_rows, 0)
    block = jnp.concatenate([refined, opening_rows(holders, positions)], axis=0)

    self_owner = lax.axis_index(("branch", "seq"))
    length = holder_utterance_length[self_owner]
    blocks = gather_blocks(block)
    block_count = blocks.shape[0]
    tags = lax.dynamic_slice(blocks, (0, half_rows, self_owner), (block_count, 3, 1))
    tags = tags[:, :, 0].astype(jnp.float32)
    places = jnp.arange(block_count, dtype=jnp.float32) * half_rows
    begin = jnp.sum(tags[:, 0] * (places + LANES * tags[:, 1] + tags[:, 2])).astype(jnp.int32)
    low = jnp.minimum(begin // half_rows, block_count - 3)
    near = lax.dynamic_slice(blocks, (low, 0, 0), (3, half_rows, LANES)).reshape(-1, LANES)
    begin = begin - low * half_rows
    first = jnp.minimum(begin, near.shape[0] - frame_count)
    holder_mel = lax.dynamic_slice_in_dim(near, first, frame_count, 0)
    utterance_frames_length = jnp.stack([length, begin - first])
    wave = vocoder_synthesize(
        holder_mel,
        utterance_frames_length,
        input_conv_weight,
        input_conv_bias,
        transposed_conv_weight,
        transposed_conv_bias,
        snake_freq_first,
        dilated_conv_weight,
        dilated_conv_bias,
        snake_freq_second,
        second_conv_weight,
        second_conv_bias,
    )
    return wave[None]


def solution(mesh):
    return jax.shard_map(
        local,
        mesh=mesh,
        in_specs=(
            P("branch", "seq", None),
            P(None, "seq"),
            P(),
            P(),
            P(),
            P(),
            P(),
            P(),
            P(),
            P(),
            P(),
            P(),
            P(),
            P(),
            P(),
            P(),
            P(),
            P(),
            P(),
            P("seq"),
            P("seq"),
            P(),
        ),
        out_specs=P(("branch", "seq"), None, None),
        check_vma=False,
    )
```
